32 devices in a mesh: comp: 16 (over z, y, core), grp: 2 (over x).
Axes of the slice: x: 2, y: 2, z: 4, core: 2. Of those that a mesh axis runs over, the one named last changes fastest.
Arguments:
- spectrum: float32 [1152, 16, 256], P('comp', 'grp'), may hold values from 0.1 to 1
- group_speed: float32 [2, 1152], replicated, may hold values from -0.25 to 0.25
- sea_mask: int32 [16, 256], P('grp'), may hold values 0 or 1
- quad_index: int32 [4, 1152], replicated, may hold values from 0 to 1151
- coupling: bfloat16 [1152, 1152], replicated, may hold values from -0.1875 to 0.1875
- stokes_kernel: float32 [32, 1152], replicated, may hold values from -0.1875 to 0.1875
- ocean_flow: float32 [2, 16, 16, 256], P(None, None, None, 'comp'), may hold values from -4 to 4
Outputs:
- forecast: float32 [1152, 16, 256], P('comp', 'grp')
- ocean_state: float32 [2, 16, 16, 256], P(None, None, None, 'comp')
The draws below stay inside these ranges and needn't reach their ends.
All inputs are finite; a program needn't handle non-finite values. No bound on the sum of `sea_mask` on one device may be relied on, other than what follows from the above.
Results may differ from the reference program's by a relative error of at most 0.0004.
Values sent between devices are 32-bit elements; how exact they have to be, the bound alone decides.
A program may use at most 64 MiB of HBM per device.

```python
import math
import jax
import jax.numpy as jnp
from jax import lax

K = 1152
Q = 1152
L = 16
STEPS = 2
SUB = 3
NY = 16
NX = 256


def touch_ends(values, stream_key, least, largest):
    dims = values.shape
    index_at = [jax.random.randint(jax.random.fold_in(stream_key, axis), (), 0, dims[axis]) for axis in range(len(dims))]
    values = values.at[tuple(index_at)].set(least)
    longest = dims.index(max(dims))
    index_at[longest] = (index_at[longest] + 1) % dims[longest]
    return values.at[tuple(index_at)].set(largest)


def block_levels(stream_key, shape, pieces, low, largest):
    gain, own = 1.0, jax.random.fold_in(stream_key, 6)
    for dim, parts in pieces:
        heights = jnp.exp(jax.random.uniform(jax.random.fold_in(own, dim), (parts,), jnp.float32, low / len(pieces), largest / len(pieces)))
        gain = gain * jnp.repeat(heights, shape[dim] // parts).reshape([-1 if axis == dim else 1 for axis in range(len(shape))])
    return gain


def centred(stream_key, dims, width, most, cuts=(), dtype=jnp.bfloat16):
    factor_of = block_levels(stream_key, dims, cuts, -0.22, 0.18) if cuts else 1.0
    drawn = jax.random.normal(stream_key, dims, jnp.float32) * width * factor_of
    return jnp.minimum(jnp.maximum(drawn, -most), most).astype(dtype)


def setup_inputs(seed: int = 0) -> dict:
    splits = jax.random.split(jax.random.key(seed), 8)
    spectrum = jnp.clip(jnp.exp(math.log(1.0) - 2.3025851 * jax.random.uniform(splits[0], (K, NY, NX), jnp.float32) ** block_levels(splits[0], (K, NY, NX), ((0, 16), (1, 2)), -0.2, 0.2)), 0.1, 1.0)
    group_speed = jnp.clip(jax.random.uniform(splits[1], (2, K), jnp.float32, -0.25, 0.25), -0.25, 0.25)
    sea_mask = touch_ends((jax.random.randint(splits[2], (NY, NX), 0, 5) < 4).astype(jnp.int32), jax.random.fold_in(splits[2], 1), 0, 1)
    quad_index = touch_ends(jax.random.randint(splits[3], (4, Q), 0, K), jax.random.fold_in(splits[3], 1), 0, K - 1).astype(jnp.int32)
    coupling = centred(splits[4], (K, Q), Q ** -0.5, 0.1875)
    stokes_kernel = centred(splits[5], (2 * L, K), K ** -0.5, 0.1875, (), jnp.float32)
    ocean_flow = centred(splits[6], (2, L, NY, NX), 1.0, 4.0, ((3, 16),), jnp.float32)
    return {"spectrum": spectrum, "group_speed": group_speed, "sea_mask": sea_mask, "quad_index": quad_index, "coupling": coupling, "stokes_kernel": stokes_kernel, "ocean_flow": ocean_flow}


SOURCE_GAIN = 0.3
CURRENT_GAIN = 0.25
CORIOLIS = 0.3
VISCOSITY = 0.15
MIXING = 0.15


def upwind(padded, energy, speed_x, speed_y, wet_cells):
    westward = padded[:, 1:-1, :-2]
    eastward = padded[:, 1:-1, 2:]
    southward = padded[:, :-2, 1:-1]
    northward = padded[:, 2:, 1:-1]
    moved = (energy - jnp.maximum(speed_x, 0.0) * (energy - westward)
             - jnp.minimum(speed_x, 0.0) * (eastward - energy)
             - jnp.maximum(speed_y, 0.0) * (energy - southward)
             - jnp.minimum(speed_y, 0.0) * (northward - energy))
    return moved * wet_cells


def sources(columns, quad_index, coupling, wet_flat):
    for substep in range(SUB):
        first = jnp.take(columns, quad_index[0], axis=0)
        second = jnp.take(columns, quad_index[1], axis=0)
        third = jnp.take(columns, quad_index[2], axis=0)
        fourth = jnp.take(columns, quad_index[3], axis=0)
        interaction = (first * second * (third + fourth) - third * fourth * (first + second)).astype(jnp.bfloat16)
        growth = jnp.dot(coupling, interaction, preferred_element_type=jnp.float32)
        columns = columns + wet_flat * (SOURCE_GAIN * growth / (1.0 + SOURCE_GAIN * jnp.abs(growth)))
    return columns


def laplace(padded, field):
    return padded[:, 1:-1, 2:] + padded[:, 1:-1, :-2] + padded[:, 2:, 1:-1] + padded[:, :-2, 1:-1] - 4.0 * field


def vertical(field):
    stacked = jnp.pad(field, ((1, 1), (0, 0), (0, 0)))
    return stacked[2:] + stacked[:-2] - 2.0 * field


def ocean_step(padded, flow, stokes):
    flow_x = flow[0]
    flow_y = flow[1]
    padded_x = padded[0]
    padded_y = padded[1]
    vortex = 0.5 * (padded_y[:, 1:-1, 2:] - padded_y[:, 1:-1, :-2]) - 0.5 * (padded_x[:, 2:, 1:-1] - padded_x[:, :-2, 1:-1])
    drift_x = stokes[0]
    drift_y = stokes[1]
    new_x = flow_x + CORIOLIS * (flow_y + drift_y) + vortex * drift_y + VISCOSITY * laplace(padded_x, flow_x) + MIXING * vertical(flow_x)
    new_y = flow_y - CORIOLIS * (flow_x + drift_x) - vortex * drift_x + VISCOSITY * laplace(padded_y, flow_y) + MIXING * vertical(flow_y)
    return jnp.stack([new_x, new_y])


def reference(spectrum, group_speed, sea_mask, quad_index, coupling, stokes_kernel, ocean_flow):
    wet_cells = (sea_mask == 1).astype(jnp.float32)
    energy = spectrum
    flow = ocean_flow
    for iteration in range(STEPS):
        drift = CURRENT_GAIN * jnp.tanh(flow[:, 0])
        speed_x = group_speed[0][:, None, None] + drift[0][None]
        speed_y = group_speed[1][:, None, None] + drift[1][None]
        padded = jnp.pad(energy, ((0, 0), (1, 1), (1, 1)))
        energy = upwind(padded, energy, speed_x, speed_y, wet_cells[None])

        def per_row(pair):
            row_energy, row_wet = pair
            updated = sources(row_energy, quad_index, coupling, row_wet[None])
            profile = jnp.dot(stokes_kernel, updated, precision=lax.Precision.HIGHEST)
            return updated, profile

        rows_first = jnp.transpose(energy, (1, 0, 2))
        updated, profiles = lax.map(per_row, (rows_first, wet_cells))
        energy = jnp.transpose(updated, (1, 0, 2))
        stokes = jnp.transpose(profiles, (1, 0, 2)).reshape(2, L, NY, NX)
        padded_flow = jnp.pad(flow, ((0, 0), (0, 0), (1, 1), (1, 1)))
        flow = ocean_step(padded_flow, flow, stokes)
    return energy, flow
```

```python
import jax
import jax.numpy as jnp
from jax import lax
from jax.experimental import pallas as pl
from jax.experimental.pallas import tpu as pltpu
from jax.sharding import PartitionSpec as P

L = 16
STEPS = 2
SUB = 3


SOURCE_GAIN = 0.3
CURRENT_GAIN = 0.25
CORIOLIS = 0.3
VISCOSITY = 0.15
MIXING = 0.15


def extended(cells, sides, width):
    for axis, dim in sides:
        count = lax.axis_size(axis)
        ends = count - 1
        head = lax.slice_in_dim(cells, 0, width, axis=dim)
        tail = lax.slice_in_dim(cells, cells.shape[dim] - width, cells.shape[dim], axis=dim)
        cells = jnp.concatenate(
            [
                lax.ppermute(tail, axis, [(i, (i + 1) % count) for i in range(ends)]),
                cells,
                lax.ppermute(head, axis, [((i + 1) % count, i) for i in range(ends)]),
            ],
            axis=dim,
        )
    return cells


def upwind(padded, energy, speed_x, speed_y, wet_cells):
    westward = padded[:, 1:-1, :-2]
    eastward = padded[:, 1:-1, 2:]
    southward = padded[:, :-2, 1:-1]
    northward = padded[:, 2:, 1:-1]
    moved = (
        energy
        - jnp.maximum(speed_x, 0.0) * (energy - westward)
        - jnp.minimum(speed_x, 0.0) * (eastward - energy)
        - jnp.maximum(speed_y, 0.0) * (energy - southward)
        - jnp.minimum(speed_y, 0.0) * (northward - energy)
    )
    return moved * wet_cells


def source_kernel(energy_ref, quad_ref, coupling_ref, stokes_ref, wet_ref, out_ref, profile_ref, onehot, parts, inter):
    channels = energy_ref.shape[0]
    quads = coupling_ref.shape[1]
    chunk = onehot.shape[1] // 4
    lane = 128
    place = lax.broadcasted_iota(jnp.int32, (lane, channels), 1)
    for start in range(0, quads, lane):
        turned = jnp.transpose(quad_ref[:, start:start + lane])
        for j in range(4):
            row = j * chunk + start % chunk
            hit = place == turned[:, j:j + 1]
            onehot[start // chunk, row:row + lane, :] = jnp.where(hit, 1.0, 0.0).astype(jnp.bfloat16)
    out_ref[...] = energy_ref[...]
    points = energy_ref.shape[1]

    def substep(_, carry):
        energy = out_ref[...]
        high = energy.astype(jnp.bfloat16)
        parts[:, :points] = high
        parts[:, points:] = (energy - high.astype(jnp.float32)).astype(jnp.bfloat16)
        for c in range(quads // chunk):
            both = jnp.dot(onehot[c], parts[...], preferred_element_type=jnp.float32)
            taken = both[:, :points] + both[:, points:]
            first, second, third, fourth = [taken[j * chunk:(j + 1) * chunk] for j in range(4)]
            inter[c * chunk:(c + 1) * chunk, :] = (
                first * second * (third + fourth) - third * fourth * (first + second)
            ).astype(jnp.bfloat16)
        growth = jnp.dot(coupling_ref[...], inter[...], preferred_element_type=jnp.float32)
        out_ref[...] = out_ref[...] + wet_ref[...] * (
            SOURCE_GAIN * growth / (1.0 + SOURCE_GAIN * jnp.abs(growth))
        )
        return carry

    lax.fori_loop(0, SUB, substep, 0)
    profile_ref[...] = jnp.dot(
        stokes_ref[...], out_ref[...], precision=lax.Precision.HIGHEST, preferred_element_type=jnp.float32
    )


def wave_sources(points, quad_index, coupling, stokes_kernel, wet_flat):
    channels, rows_local, cols_local = points.shape
    columns = points.reshape(channels, rows_local * cols_local)
    quads = coupling.shape[1]
    chunk = 384 if quads % 384 == 0 else quads
    vmem = pl.BlockSpec(memory_space=pltpu.VMEM)
    lanes = columns.shape[1]
    columns, profile = pl.pallas_call(
        source_kernel,
        out_shape=(
            jax.ShapeDtypeStruct(columns.shape, jnp.float32),
            jax.ShapeDtypeStruct((stokes_kernel.shape[0], lanes), jnp.float32),
        ),
        in_specs=[vmem] * 5,
        out_specs=(vmem, vmem),
        scratch_shapes=[
            pltpu.VMEM((quads // chunk, 4 * chunk, channels), jnp.bfloat16),
            pltpu.VMEM((channels, 2 * lanes), jnp.bfloat16),
            pltpu.VMEM((quads, lanes), jnp.bfloat16),
        ],
        compiler_params=pltpu.CompilerParams(vmem_limit_bytes=48 * 1024 * 1024),
    )(columns, jnp.concatenate([quad_index, quad_index]), coupling, stokes_kernel, wet_flat)
    return (columns.reshape(points.shape), profile.reshape(2, L, rows_local, cols_local))


def laplace(padded, field):
    return (
        padded[:, 1:-1, 2:]
        + padded[:, 1:-1, :-2]
        + padded[:, 2:, 1:-1]
        + padded[:, :-2, 1:-1]
        - 4.0 * field
    )


def vertical(field):
    stacked = jnp.pad(field, ((1, 1), (0, 0), (0, 0)))
    return stacked[2:] + stacked[:-2] - 2.0 * field


def ocean_step(padded, flow, stokes):
    flow_x = flow[0]
    flow_y = flow[1]
    padded_x = padded[0]
    padded_y = padded[1]
    vortex = 0.5 * (padded_y[:, 1:-1, 2:] - padded_y[:, 1:-1, :-2]) - 0.5 * (
        padded_x[:, 2:, 1:-1] - padded_x[:, :-2, 1:-1]
    )
    drift_x = stokes[0]
    drift_y = stokes[1]
    new_x = (
        flow_x
        + CORIOLIS * (flow_y + drift_y)
        + vortex * drift_y
        + VISCOSITY * laplace(padded_x, flow_x)
        + MIXING * vertical(flow_x)
    )
    new_y = (
        flow_y
        - CORIOLIS * (flow_x + drift_x)
        - vortex * drift_x
        + VISCOSITY * laplace(padded_y, flow_y)
        + MIXING * vertical(flow_y)
    )
    return jnp.stack([new_x, new_y])


def local(spectrum, group_speed, sea_mask, quad_index, coupling, stokes_kernel, ocean_flow):
    rows_local = sea_mask.shape[0]
    cols_local = ocean_flow.shape[3]
    comp_place = lax.axis_index("comp")
    group_place = lax.axis_index("grp")
    wet_rows = (sea_mask == 1).astype(jnp.float32)
    wet_tile = lax.dynamic_slice_in_dim(wet_rows, comp_place * cols_local, cols_local, 1)
    wet_flat = wet_tile.reshape(1, rows_local * cols_local)
    flow = ocean_flow
    points = lax.all_to_all(spectrum, "comp", split_axis=2, concat_axis=0, tiled=True)
    for iteration in range(STEPS):
        top_level = lax.dynamic_slice_in_dim(flow[:, 0], group_place * rows_local, rows_local, 1)
        drift = CURRENT_GAIN * jnp.tanh(top_level)
        padded = extended(points, (("comp", 2), ("grp", 1)), 1)
        speed_x = group_speed[0][:, None, None] + drift[0][None]
        speed_y = group_speed[1][:, None, None] + drift[1][None]
        points = upwind(padded, points, speed_x, speed_y, wet_tile[None])
        points, stokes = wave_sources(points, quad_index, coupling, stokes_kernel, wet_flat)
        whole_stokes = lax.all_gather(stokes, "grp", axis=2, tiled=True)
        advance_padded = extended(flow, (("comp", 3),), 1)
        advance_padded = jnp.pad(advance_padded, ((0, 0), (0, 0), (1, 1), (0, 0)))
        result = ocean_step(advance_padded, flow, whole_stokes)
        flow = result
    energy = lax.all_to_all(points, "comp", split_axis=0, concat_axis=2, tiled=True)
    return (energy, flow)


def solution(mesh):
    in_specs = (
        P("comp", "grp", None),
        P(),
        P("grp", None),
        P(),
        P(),
        P(),
        P(None, None, None, "comp"),
    )
    out_specs = (P("comp", "grp", None), P(None, None, None, "comp"))
    return jax.shard_map(local, mesh=mesh, in_specs=in_specs, out_specs=out_specs, check_vma=False)
```

```python
import functools

import jax
import jax.numpy as jnp
from jax import lax
from jax.experimental import pallas as pl
from jax.experimental.pallas import tpu as pltpu
from jax.sharding import PartitionSpec as P

L = 16
STEPS = 2
SUB = 3


SOURCE_GAIN = 0.3
CURRENT_GAIN = 0.25
CORIOLIS = 0.3
VISCOSITY = 0.15
MIXING = 0.15


MESH = pl.DeviceIdType.MESH


def upwind(energy, westward, eastward, southward, northward, speed_x, speed_y, wet_cells):
    moved = (
        energy
        - jnp.maximum(speed_x, 0.0) * (energy - westward)
        - jnp.minimum(speed_x, 0.0) * (eastward - energy)
        - jnp.maximum(speed_y, 0.0) * (energy - southward)
        - jnp.minimum(speed_y, 0.0) * (northward - energy)
    )
    return moved * wet_cells


def shifted(values, step, axis):
    return pltpu.roll(values, step % values.shape[axis], axis)


def swap_blocks(values):
    count, lanes = values.shape[-2:]
    width = lanes // count
    down, across = values.ndim - 2, values.ndim - 1
    s = lax.broadcasted_iota(jnp.int32, values.shape, down)
    l = lax.broadcasted_iota(jnp.int32, values.shape, across) // width
    step = 1
    while step < count:
        s_bit, l_bit = (s // step) % 2, (l // step) % 2
        upper = shifted(shifted(values, -step, down), step * width, across)
        lower = shifted(shifted(values, step, down), -step * width, across)
        values = jnp.where(s_bit == l_bit, values, jnp.where(s_bit == 0, upper, lower))
        step *= 2
    return values


def greet(n, g, me, gp, everyone):
    barrier = pltpu.get_barrier_semaphore()
    others = range(1, n) if everyone else (1, n - 1)
    for i in others:
        pl.semaphore_signal(barrier, inc=1, device_id=(lax.rem(me + i, n), gp), device_id_type=MESH)
    for i in range(1, g):
        pl.semaphore_signal(barrier, inc=1, device_id=(me, lax.rem(gp + i, g)), device_id_type=MESH)
    pl.semaphore_wait(barrier, len(others) + g - 1)


def remote(src, dst, send, recv, device):
    return pltpu.make_async_remote_copy(
        src_ref=src, dst_ref=dst, send_sem=send, recv_sem=recv, device_id=device, device_id_type=MESH
    )


def enter_kernel(n, g, spectrum_ref, flow_ref, speed_ref, mask_ref, out_ref,
                 south, north, drift_out, drift_in, blocks, sends, recvs, halo_sems):
    me, gp = lax.axis_index("comp"), lax.axis_index("grp")
    kept, rows, cols = spectrum_ref.shape
    lanes = blocks.shape[2]
    levels = flow_ref.shape[0] // 2
    greet(n, g, me, gp, True)
    up, down = lax.rem(gp + 1, g), lax.rem(gp + g - 1, g)
    to_up = remote(spectrum_ref.at[:, rows - 1, :], south.at[:, rows - 1, :], halo_sems.at[0], halo_sems.at[1], (me, up))
    to_down = remote(spectrum_ref.at[:, 0, :], north.at[:, 0, :], halo_sems.at[2], halo_sems.at[3], (me, down))
    to_up.start()
    to_down.start()
    here = pl.ds(pl.multiple_of(gp * lanes, lanes), lanes)
    drift_out[0:1, :] = CURRENT_GAIN * jnp.tanh(flow_ref[0:1, here])
    drift_out[1:2, :] = CURRENT_GAIN * jnp.tanh(flow_ref[levels:levels + 1, here])
    drift_in[me] = drift_out[...]
    for i in range(1, n):
        peer = lax.rem(me + i, n)
        remote(drift_out, drift_in.at[me], sends.at[0, peer], recvs.at[0, me], (peer, gp)).start()
    energy = spectrum_ref[...]
    row = lax.broadcasted_iota(jnp.int32, energy.shape, 1)
    col = lax.broadcasted_iota(jnp.int32, energy.shape, 2)
    westward = jnp.where(col == 0, 0.0, shifted(energy, 1, 2))
    eastward = jnp.where(col == cols - 1, 0.0, shifted(energy, -1, 2))
    to_up.wait()
    to_down.wait()
    below = jnp.where(gp == 0, 0.0, 1.0) * south[:, rows - 1:rows, :]
    above = jnp.where(gp == g - 1, 0.0, 1.0) * north[:, 0:1, :]
    southward = jnp.where(row == 0, below, shifted(energy, 1, 1))
    northward = jnp.where(row == rows - 1, above, shifted(energy, -1, 1))
    for i in range(1, n):
        peer = lax.rem(me + i, n)
        remote(drift_out, drift_in.at[peer], sends.at[0, peer], recvs.at[0, peer], (peer, gp)).wait()
    wet = (mask_ref[...] == 1).astype(jnp.float32)
    for h in range(cols // lanes):
        part = slice(h * lanes, (h + 1) * lanes)
        drift_x = swap_blocks(drift_in[h * rows:(h + 1) * rows, 0, :])
        drift_y = swap_blocks(drift_in[h * rows:(h + 1) * rows, 1, :])
        moved = upwind(
            energy[:, :, part], westward[:, :, part], eastward[:, :, part],
            southward[:, :, part], northward[:, :, part],
            speed_ref[0] + drift_x[None], speed_ref[1] + drift_y[None], wet[None, :, part],
        )
        blocks[h * rows:(h + 1) * rows] = jnp.swapaxes(swap_blocks(moved), 0, 1)
    for i in range(1, n):
        peer = lax.rem(me + i, n)
        remote(blocks.at[peer], out_ref.at[me], sends.at[1, peer], recvs.at[1, me], (peer, gp)).start()
    out_ref[me] = blocks[me]
    for i in range(1, n):
        peer = lax.rem(me + i, n)
        remote(blocks.at[peer], out_ref.at[peer], sends.at[1, peer], recvs.at[1, peer], (peer, gp)).wait()


def column_upwind(height, energy, halo_ref, pick_ref, speed_ref, drift_ref, wet):
    rows = halo_ref.shape[0]
    width = rows // 2 - height
    lanes = energy.shape[1]
    place = lax.broadcasted_iota(jnp.int32, (1, lanes), 1)
    turned = jnp.transpose(halo_ref[...])
    sides = 2 * height
    lateral = jnp.dot(turned[:, :sides], pick_ref[:sides, :], precision=lax.Precision.HIGHEST, preferred_element_type=jnp.float32)
    polar = jnp.dot(turned[:, sides:rows], pick_ref[sides:rows, :], precision=lax.Precision.HIGHEST, preferred_element_type=jnp.float32)
    col = place % width
    westward = jnp.where(col == 0, lateral, shifted(energy, 1, 1))
    eastward = jnp.where(col == width - 1, lateral, shifted(energy, -1, 1))
    southward = jnp.where(place < width, polar, shifted(energy, width, 1))
    northward = jnp.where(place >= lanes - width, polar, shifted(energy, -width, 1))
    return upwind(
        energy, westward, eastward, southward, northward,
        speed_ref[:, 0:1] + drift_ref[0:1, :], speed_ref[:, 1:2] + drift_ref[1:2, :], wet,
    )


def source_kernel(advect, height, energy_ref, quad_ref, coupling_ref, stokes_ref, wet_ref, pick_ref, *refs):
    if advect:
        halo_ref, speed_ref, drift_ref, *refs = refs
        out_ref, profile_ref, onehot, parts, inter = refs
    else:
        out_ref, profile_ref, edge_ref, onehot, parts, inter = refs
    channels = energy_ref.shape[0]
    quads = coupling_ref.shape[1]
    chunk = onehot.shape[1] // 4
    lane = 128
    place = lax.broadcasted_iota(jnp.int32, (lane, channels), 1)
    for start in range(0, quads, lane):
        turned = jnp.transpose(quad_ref[:, start:start + lane])
        for j in range(4):
            row = j * chunk + start % chunk
            hit = place == turned[:, j:j + 1]
            onehot[start // chunk, row:row + lane, :] = jnp.where(hit, 1.0, 0.0).astype(jnp.bfloat16)
    points = energy_ref.shape[1]
    if advect:
        out_ref[...] = column_upwind(
            height, energy_ref[...], halo_ref, pick_ref, speed_ref, drift_ref, wet_ref[...]
        )
    else:
        out_ref[...] = energy_ref[...]

    def substep(_, carry):
        energy = out_ref[...]
        high = energy.astype(jnp.bfloat16)
        parts[:, :points] = high
        parts[:, points:] = (energy - high.astype(jnp.float32)).astype(jnp.bfloat16)
        for c in range(quads // chunk):
            both = jnp.dot(onehot[c], parts[...], preferred_element_type=jnp.float32)
            taken = both[:, :points] + both[:, points:]
            first, second, third, fourth = [taken[j * chunk:(j + 1) * chunk] for j in range(4)]
            inter[c * chunk:(c + 1) * chunk, :] = (
                first * second * (third + fourth) - third * fourth * (first + second)
            ).astype(jnp.bfloat16)
        growth = jnp.dot(coupling_ref[...], inter[...], preferred_element_type=jnp.float32)
        out_ref[...] = out_ref[...] + wet_ref[...] * (
            SOURCE_GAIN * growth / (1.0 + SOURCE_GAIN * jnp.abs(growth))
        )
        return carry

    lax.fori_loop(0, SUB, substep, 0)
    profile_ref[...] = jnp.dot(
        stokes_ref[...], out_ref[...], precision=lax.Precision.HIGHEST, preferred_element_type=jnp.float32
    )
    if not advect:
        edge_ref[...] = lax.dot_general(
            pick_ref[...], out_ref[...], (((1,), (1,)), ((), ())),
            precision=lax.Precision.HIGHEST, preferred_element_type=jnp.float32,
        )


def ocean_step(width, flow, west_flow, east_flow, stokes, first, last):
    levels = flow.shape[0] // 2
    size = flow.shape[1]
    place = lax.broadcasted_iota(jnp.int32, flow.shape, 1)
    col = place % width
    level = lax.broadcasted_iota(jnp.int32, (levels, size), 0)
    west_edge = jnp.where(first, 0.0, shifted(west_flow, 1 - width, 1))
    east_edge = jnp.where(last, 0.0, shifted(east_flow, width - 1, 1))
    west = jnp.where(col == 0, west_edge, shifted(flow, 1, 1))
    east = jnp.where(col == width - 1, east_edge, shifted(flow, -1, 1))
    south = jnp.where(place < width, 0.0, shifted(flow, width, 1))
    north = jnp.where(place >= size - width, 0.0, shifted(flow, -width, 1))
    lap = east + west + north + south - 4.0 * flow
    u, v = flow[:levels], flow[levels:]

    def vertical(field):
        higher = jnp.where(level == 0, 0.0, shifted(field, 1, 0))
        lower = jnp.where(level == levels - 1, 0.0, shifted(field, -1, 0))
        return lower + higher - 2.0 * field

    vortex = 0.5 * (east[levels:] - west[levels:]) - 0.5 * (north[:levels] - south[:levels])
    drift_x, drift_y = stokes[:levels], stokes[levels:]
    new_x = u + CORIOLIS * (v + drift_y) + vortex * drift_y + VISCOSITY * lap[:levels] + MIXING * vertical(u)
    new_y = v - CORIOLIS * (u + drift_x) - vortex * drift_x + VISCOSITY * lap[levels:] + MIXING * vertical(v)
    return new_x, new_y


def ocean_copies(n, g, me, gp, flow_ref, profile_ref, west_flow, east_flow, stokes_all, sems, psend, precv):
    right, left = lax.rem(me + 1, n), lax.rem(me + n - 1, n)
    starts = [
        remote(flow_ref, west_flow, sems.at[0], sems.at[1], (right, gp)),
        remote(flow_ref, east_flow, sems.at[2], sems.at[3], (left, gp)),
    ]
    waits = list(starts)
    for i in range(1, g):
        peer = lax.rem(gp + i, g)
        starts.append(remote(profile_ref, stokes_all.at[gp], psend.at[peer], precv.at[gp], (me, peer)))
        waits.append(remote(profile_ref, stokes_all.at[peer], psend.at[peer], precv.at[peer], (me, peer)))
    for copy in starts:
        copy.start()
    stokes_all[gp] = profile_ref[...]
    return waits


def middle_kernel(n, g, width, flow_ref, profile_ref, edge_ref, flow_out, drift_out, halo_out,
                  west_flow, east_flow, stokes_all, halo, sems, psend, precv, halo_sems):
    me, gp = lax.axis_index("comp"), lax.axis_index("grp")
    levels = flow_ref.shape[0] // 2
    lanes = profile_ref.shape[1]
    height = lanes // width
    greet(n, g, me, gp, False)
    right, left = lax.rem(me + 1, n), lax.rem(me + n - 1, n)
    up, down = lax.rem(gp + 1, g), lax.rem(gp + g - 1, g)
    a, b, c, d = height, 2 * height, 2 * height + width, 2 * height + 2 * width
    waits = ocean_copies(n, g, me, gp, flow_ref, profile_ref, west_flow, east_flow, stokes_all, sems, psend, precv)
    moves = [
        remote(edge_ref.at[a:b], halo.at[0:a], halo_sems.at[0], halo_sems.at[1], (right, gp)),
        remote(edge_ref.at[0:a], halo.at[a:b], halo_sems.at[2], halo_sems.at[3], (left, gp)),
        remote(edge_ref.at[c:d], halo.at[b:c], halo_sems.at[4], halo_sems.at[5], (me, up)),
        remote(edge_ref.at[b:c], halo.at[c:d], halo_sems.at[6], halo_sems.at[7], (me, down)),
    ]
    for copy in moves:
        copy.start()
    for copy in waits:
        copy.wait()
    stokes = jnp.concatenate([stokes_all[i] for i in range(g)], axis=1)
    new_x, new_y = ocean_step(width, flow_ref[...], west_flow[...], east_flow[...], stokes, me == 0, me == n - 1)
    flow_out[:levels, :] = new_x
    flow_out[levels:, :] = new_y
    here = pl.ds(pl.multiple_of(gp * lanes, lanes), lanes)
    drift_out[0:1, :] = CURRENT_GAIN * jnp.tanh(flow_out[0:1, here])
    drift_out[1:2, :] = CURRENT_GAIN * jnp.tanh(flow_out[levels:levels + 1, here])
    for copy in moves:
        copy.wait()
    halo_out[0:a, :] = jnp.where(me == 0, 0.0, halo[0:a, :])
    halo_out[a:b, :] = jnp.where(me == n - 1, 0.0, halo[a:b, :])
    halo_out[b:c, :] = jnp.where(gp == 0, 0.0, halo[b:c, :])
    halo_out[c:d, :] = jnp.where(gp == g - 1, 0.0, halo[c:d, :])


def exit_kernel(n, g, width, points_ref, flow_ref, profile_ref, out_ref, flow_out,
                west_flow, east_flow, stokes_all, blocks, sems, psend, precv, sends, recvs):
    me, gp = lax.axis_index("comp"), lax.axis_index("grp")
    levels = flow_ref.shape[0] // 2
    kept, rows, cols = out_ref.shape
    lanes = blocks.shape[2]
    greet(n, g, me, gp, True)
    waits = ocean_copies(n, g, me, gp, flow_ref, profile_ref, west_flow, east_flow, stokes_all, sems, psend, precv)
    for i in range(1, n):
        peer = lax.rem(me + i, n)
        remote(points_ref.at[peer], blocks.at[me], sends.at[peer], recvs.at[me], (peer, gp)).start()
    blocks[me] = points_ref[me]
    for copy in waits:
        copy.wait()
    stokes = jnp.concatenate([stokes_all[i] for i in range(g)], axis=1)
    new_x, new_y = ocean_step(width, flow_ref[...], west_flow[...], east_flow[...], stokes, me == 0, me == n - 1)
    flow_out[:levels, :] = new_x
    flow_out[levels:, :] = new_y
    for i in range(1, n):
        peer = lax.rem(me + i, n)
        remote(points_ref.at[peer], blocks.at[peer], sends.at[peer], recvs.at[peer], (peer, gp)).wait()
    for h in range(cols // lanes):
        turned = jnp.swapaxes(blocks[h * rows:(h + 1) * rows], 0, 1)
        out_ref[:, :, h * lanes:(h + 1) * lanes] = swap_blocks(turned)


VMEM = pltpu.VMEM
DMA = pltpu.SemaphoreType.DMA


def call(kernel, operands, outs, scratch, collective=None):
    whole = pl.BlockSpec(memory_space=pltpu.VMEM)
    extra = {} if collective is None else {"collective_id": collective, "has_side_effects": True}
    return pl.pallas_call(
        kernel,
        out_shape=tuple(jax.ShapeDtypeStruct(shape, jnp.float32) for shape in outs),
        in_specs=[whole] * len(operands),
        out_specs=(whole,) * len(outs),
        scratch_shapes=scratch,
        compiler_params=pltpu.CompilerParams(vmem_limit_bytes=48 * 1024 * 1024, **extra),
    )(*operands)


def local(spectrum, group_speed, sea_mask, quad_index, coupling, stokes_kernel, ocean_flow):
    f32 = jnp.float32
    n, g = lax.axis_size("comp"), lax.axis_size("grp")
    kept, rows, cols = spectrum.shape
    width = ocean_flow.shape[3]
    lanes = rows * width
    channels, quads = coupling.shape
    place = lax.axis_index("comp")
    flow = ocean_flow.reshape(2 * L, -1)
    deep, size = flow.shape
    own = lax.dynamic_slice_in_dim(group_speed, place * kept, kept, 1)
    own = jnp.broadcast_to(own[:, :, None, None], (2, kept, rows, lanes))
    wet_flat = (lax.dynamic_slice_in_dim(sea_mask, place * width, width, 1) == 1).astype(f32).reshape(1, lanes)
    quad = jnp.concatenate([quad_index, quad_index])
    lane = jnp.arange(lanes)
    rank = jnp.arange(rows)[:, None]
    across = jnp.arange(width)[:, None]
    pick = jnp.concatenate([
        lane == rank * width, lane == rank * width + width - 1, lane == across, lane == lanes - width + across,
    ]).astype(f32)
    edges = pick.shape[0]
    chunk = 384 if quads % 384 == 0 else quads
    work = [
        VMEM((quads // chunk, 4 * chunk, channels), jnp.bfloat16),
        VMEM((channels, 2 * lanes), jnp.bfloat16),
        VMEM((quads, lanes), jnp.bfloat16),
    ]
    sea = [VMEM((deep, size), f32), VMEM((deep, size), f32), VMEM((g, deep, lanes), f32)]

    (points,) = call(
        functools.partial(enter_kernel, n, g), (spectrum, flow, own, sea_mask), ((n, kept, lanes),),
        [VMEM((kept, rows, cols), f32), VMEM((kept, rows, cols), f32), VMEM((2, lanes), f32),
         VMEM((n, 2, lanes), f32), VMEM((n, kept, lanes), f32), DMA((2, n)), DMA((2, n)), DMA((4,))], 0,
    )
    fixed = (quad, coupling, stokes_kernel, wet_flat, pick)
    points, profile, edge = call(
        functools.partial(source_kernel, False, rows), (points.reshape(channels, lanes), *fixed),
        ((channels, lanes), (deep, lanes), (edges, channels)), work,
    )
    flow, drift, halo = call(
        functools.partial(middle_kernel, n, g, width), (flow, profile, edge),
        ((deep, size), (2, lanes), (edges, channels)),
        sea + [VMEM((edges, channels), f32), DMA((4,)), DMA((g,)), DMA((g,)), DMA((8,))], 1,
    )
    points, profile = call(
        functools.partial(source_kernel, True, rows), (points, *fixed, halo, group_speed.T, drift),
        ((channels, lanes), (deep, lanes)), work,
    )
    energy, flow = call(
        functools.partial(exit_kernel, n, g, width), (points.reshape(n, kept, lanes), flow, profile),
        ((kept, rows, cols), (deep, size)),
        sea + [VMEM((n, kept, lanes), f32), DMA((4,)), DMA((g,)), DMA((g,)), DMA((n,)), DMA((n,))], 2,
    )
    return (energy, flow.reshape(ocean_flow.shape))


def solution(mesh):
    in_specs = (
        P("comp", "grp", None),
        P(),
        P("grp", None),
        P(),
        P(),
        P(),
        P(None, None, None, "comp"),
    )
    out_specs = (P("comp", "grp", None), P(None, None, None, "comp"))
    return jax.shard_map(local, mesh=mesh, in_specs=in_specs, out_specs=out_specs, check_vma=False)
```

```python
import functools

import jax
import jax.numpy as jnp
from jax import lax
from jax.experimental import pallas as pl
from jax.experimental.pallas import tpu as pltpu
from jax.sharding import PartitionSpec as P

L = 16
STEPS = 2
SUB = 3


SOURCE_GAIN = 0.3
CURRENT_GAIN = 0.25
CORIOLIS = 0.3
VISCOSITY = 0.15
MIXING = 0.15


MESH = pl.DeviceIdType.MESH


def upwind(energy, westward, eastward, southward, northward, speed_x, speed_y, wet_cells):
    moved = (
        energy
        - jnp.maximum(speed_x, 0.0) * (energy - westward)
        - jnp.minimum(speed_x, 0.0) * (eastward - energy)
        - jnp.maximum(speed_y, 0.0) * (energy - southward)
        - jnp.minimum(speed_y, 0.0) * (northward - energy)
    )
    return moved * wet_cells


def shifted(values, step, axis):
    return pltpu.roll(values, step % values.shape[axis], axis)


def swap_blocks(values):
    count, lanes = values.shape[-2:]
    width = lanes // count
    down, across = values.ndim - 2, values.ndim - 1
    s = lax.broadcasted_iota(jnp.int32, values.shape, down)
    l = lax.broadcasted_iota(jnp.int32, values.shape, across) // width
    step = 1
    while step < count:
        s_bit, l_bit = (s // step) % 2, (l // step) % 2
        upper = shifted(shifted(values, -step, down), step * width, across)
        lower = shifted(shifted(values, step, down), -step * width, across)
        values = jnp.where(s_bit == l_bit, values, jnp.where(s_bit == 0, upper, lower))
        step *= 2
    return values


def greet(n, g, me, gp, everyone):
    barrier = pltpu.get_barrier_semaphore()
    others = range(1, n) if everyone else (1, n - 1)
    for i in others:
        pl.semaphore_signal(barrier, inc=1, device_id=(lax.rem(me + i, n), gp), device_id_type=MESH)
    for i in range(1, g):
        pl.semaphore_signal(barrier, inc=1, device_id=(me, lax.rem(gp + i, g)), device_id_type=MESH)
    pl.semaphore_wait(barrier, len(others) + g - 1)


def remote(src, dst, send, recv, device):
    return pltpu.make_async_remote_copy(
        src_ref=src, dst_ref=dst, send_sem=send, recv_sem=recv, device_id=device, device_id_type=MESH
    )


def enter_kernel(n, g, spectrum_ref, flow_ref, speed_ref, mask_ref, out_ref,
                 south, north, drift_out, drift_in, blocks, sends, recvs, halo_sems):
    me, gp = lax.axis_index("comp"), lax.axis_index("grp")
    kept, rows, cols = spectrum_ref.shape
    lanes = blocks.shape[2]
    levels = flow_ref.shape[0] // 2
    greet(n, g, me, gp, True)
    up, down = lax.rem(gp + 1, g), lax.rem(gp + g - 1, g)
    to_up = remote(spectrum_ref.at[:, rows - 1, :], south.at[:, rows - 1, :], halo_sems.at[0], halo_sems.at[1], (me, up))
    to_down = remote(spectrum_ref.at[:, 0, :], north.at[:, 0, :], halo_sems.at[2], halo_sems.at[3], (me, down))
    to_up.start()
    to_down.start()
    here = pl.ds(pl.multiple_of(gp * lanes, lanes), lanes)
    drift_out[0:1, :] = CURRENT_GAIN * jnp.tanh(flow_ref[0:1, here])
    drift_out[1:2, :] = CURRENT_GAIN * jnp.tanh(flow_ref[levels:levels + 1, here])
    drift_in[me] = drift_out[...]
    for i in range(1, n):
        peer = lax.rem(me + i, n)
        remote(drift_out, drift_in.at[me], sends.at[0, peer], recvs.at[0, me], (peer, gp)).start()
    energy = spectrum_ref[...]
    row = lax.broadcasted_iota(jnp.int32, energy.shape, 1)
    col = lax.broadcasted_iota(jnp.int32, energy.shape, 2)
    westward = jnp.where(col == 0, 0.0, shifted(energy, 1, 2))
    eastward = jnp.where(col == cols - 1, 0.0, shifted(energy, -1, 2))
    to_up.wait()
    to_down.wait()
    below = jnp.where(gp == 0, 0.0, 1.0) * south[:, rows - 1:rows, :]
    above = jnp.where(gp == g - 1, 0.0, 1.0) * north[:, 0:1, :]
    southward = jnp.where(row == 0, below, shifted(energy, 1, 1))
    northward = jnp.where(row == rows - 1, above, shifted(energy, -1, 1))
    for i in range(1, n):
        peer = lax.rem(me + i, n)
        remote(drift_out, drift_in.at[peer], sends.at[0, peer], recvs.at[0, peer], (peer, gp)).wait()
    wet = (mask_ref[...] == 1).astype(jnp.float32)
    for h in range(cols // lanes):
        part = slice(h * lanes, (h + 1) * lanes)
        drift_x = swap_blocks(drift_in[h * rows:(h + 1) * rows, 0, :])
        drift_y = swap_blocks(drift_in[h * rows:(h + 1) * rows, 1, :])
        moved = upwind(
            energy[:, :, part], westward[:, :, part], eastward[:, :, part],
            southward[:, :, part], northward[:, :, part],
            speed_ref[0] + drift_x[None], speed_ref[1] + drift_y[None], wet[None, :, part],
        )
        blocks[h * rows:(h + 1) * rows] = jnp.swapaxes(swap_blocks(moved), 0, 1)
    for i in range(1, n):
        peer = lax.rem(me + i, n)
        remote(blocks.at[peer], out_ref.at[me], sends.at[1, peer], recvs.at[1, me], (peer, gp)).start()
    out_ref[me] = blocks[me]
    for i in range(1, n):
        peer = lax.rem(me + i, n)
        remote(blocks.at[peer], out_ref.at[peer], sends.at[1, peer], recvs.at[1, peer], (peer, gp)).wait()


def edge_pick(height, lanes):
    width = lanes // height
    shape = (2 * height + 2 * width, lanes)
    k = lax.broadcasted_iota(jnp.int32, shape, 0)
    east = (k - height) * width + width - 1
    south = k - 2 * height
    north = lanes - width + south - width
    lane = jnp.where(
        k < height, k * width, jnp.where(k < 2 * height, east, jnp.where(south < width, south, north))
    )
    return jnp.where(lax.broadcasted_iota(jnp.int32, shape, 1) == lane, 1.0, 0.0)


def column_upwind(height, energy, halo_ref, pick, speed_ref, drift_ref, wet):
    rows = halo_ref.shape[0]
    width = rows // 2 - height
    lanes = energy.shape[1]
    place = lax.broadcasted_iota(jnp.int32, (1, lanes), 1)
    turned = jnp.transpose(halo_ref[...])
    sides = 2 * height
    lateral = jnp.dot(turned[:, :sides], pick[:sides], precision=lax.Precision.HIGHEST, preferred_element_type=jnp.float32)
    polar = jnp.dot(turned[:, sides:rows], pick[sides:rows], precision=lax.Precision.HIGHEST, preferred_element_type=jnp.float32)
    col = place % width
    westward = jnp.where(col == 0, lateral, shifted(energy, 1, 1))
    eastward = jnp.where(col == width - 1, lateral, shifted(energy, -1, 1))
    southward = jnp.where(place < width, polar, shifted(energy, width, 1))
    northward = jnp.where(place >= lanes - width, polar, shifted(energy, -width, 1))
    return upwind(
        energy, westward, eastward, southward, northward,
        speed_ref[:, 0:1] + drift_ref[0:1, :], speed_ref[:, 1:2] + drift_ref[1:2, :], wet,
    )


def source_kernel(advect, height, energy_ref, quad_ref, coupling_ref, stokes_ref, wet_ref, *refs):
    if advect:
        halo_ref, speed_ref, drift_ref, *refs = refs
        out_ref, profile_ref, onehot, parts, inter = refs
    else:
        out_ref, profile_ref, edge_ref, onehot, parts, inter = refs
    channels = energy_ref.shape[0]
    quads = coupling_ref.shape[1]
    chunk = onehot.shape[1] // 4
    lane = 128
    place = lax.broadcasted_iota(jnp.int32, (lane, channels), 1)
    quad = jnp.concatenate([quad_ref[...], quad_ref[...]], axis=0)
    pick = edge_pick(height, energy_ref.shape[1])
    for start in range(0, quads, lane):
        turned = jnp.transpose(quad[:, start:start + lane])
        for j in range(4):
            row = j * chunk + start % chunk
            hit = place == turned[:, j:j + 1]
            onehot[start // chunk, row:row + lane, :] = jnp.where(hit, 1.0, 0.0).astype(jnp.bfloat16)
    points = energy_ref.shape[1]
    if advect:
        out_ref[...] = column_upwind(
            height, energy_ref[...], halo_ref, pick, speed_ref, drift_ref, wet_ref[...]
        )
    else:
        out_ref[...] = energy_ref[...]

    def substep(_, carry):
        energy = out_ref[...]
        high = energy.astype(jnp.bfloat16)
        parts[:, :points] = high
        parts[:, points:] = (energy - high.astype(jnp.float32)).astype(jnp.bfloat16)
        for c in range(quads // chunk):
            both = jnp.dot(onehot[c], parts[...], preferred_element_type=jnp.float32)
            taken = both[:, :points] + both[:, points:]
            first, second, third, fourth = [taken[j * chunk:(j + 1) * chunk] for j in range(4)]
            inter[c * chunk:(c + 1) * chunk, :] = (
                first * second * (third + fourth) - third * fourth * (first + second)
            ).astype(jnp.bfloat16)
        growth = jnp.dot(coupling_ref[...], inter[...], preferred_element_type=jnp.float32)
        out_ref[...] = out_ref[...] + wet_ref[...] * (
            SOURCE_GAIN * growth / (1.0 + SOURCE_GAIN * jnp.abs(growth))
        )
        return carry

    lax.fori_loop(0, SUB, substep, 0)
    profile_ref[...] = jnp.dot(
        stokes_ref[...], out_ref[...], precision=lax.Precision.HIGHEST, preferred_element_type=jnp.float32
    )
    if not advect:
        edge_ref[...] = lax.dot_general(
            pick, out_ref[...], (((1,), (1,)), ((), ())),
            precision=lax.Precision.HIGHEST, preferred_element_type=jnp.float32,
        )


def ocean_step(width, flow, west_flow, east_flow, stokes, first, last):
    levels = flow.shape[0] // 2
    size = flow.shape[1]
    place = lax.broadcasted_iota(jnp.int32, flow.shape, 1)
    col = place % width
    level = lax.broadcasted_iota(jnp.int32, (levels, size), 0)
    west_edge = jnp.where(first, 0.0, shifted(west_flow, 1 - width, 1))
    east_edge = jnp.where(last, 0.0, shifted(east_flow, width - 1, 1))
    west = jnp.where(col == 0, west_edge, shifted(flow, 1, 1))
    east = jnp.where(col == width - 1, east_edge, shifted(flow, -1, 1))
    south = jnp.where(place < width, 0.0, shifted(flow, width, 1))
    north = jnp.where(place >= size - width, 0.0, shifted(flow, -width, 1))
    lap = east + west + north + south - 4.0 * flow
    u, v = flow[:levels], flow[levels:]

    def vertical(field):
        higher = jnp.where(level == 0, 0.0, shifted(field, 1, 0))
        lower = jnp.where(level == levels - 1, 0.0, shifted(field, -1, 0))
        return lower + higher - 2.0 * field

    vortex = 0.5 * (east[levels:] - west[levels:]) - 0.5 * (north[:levels] - south[:levels])
    drift_x, drift_y = stokes[:levels], stokes[levels:]
    new_x = u + CORIOLIS * (v + drift_y) + vortex * drift_y + VISCOSITY * lap[:levels] + MIXING * vertical(u)
    new_y = v - CORIOLIS * (u + drift_x) - vortex * drift_x + VISCOSITY * lap[levels:] + MIXING * vertical(v)
    return new_x, new_y


def ocean_copies(n, g, me, gp, flow_ref, profile_ref, west_flow, east_flow, stokes_all, sems, psend, precv):
    right, left = lax.rem(me + 1, n), lax.rem(me + n - 1, n)
    starts = [
        remote(flow_ref, west_flow, sems.at[0], sems.at[1], (right, gp)),
        remote(flow_ref, east_flow, sems.at[2], sems.at[3], (left, gp)),
    ]
    waits = list(starts)
    for i in range(1, g):
        peer = lax.rem(gp + i, g)
        starts.append(remote(profile_ref, stokes_all.at[gp], psend.at[peer], precv.at[gp], (me, peer)))
        waits.append(remote(profile_ref, stokes_all.at[peer], psend.at[peer], precv.at[peer], (me, peer)))
    for copy in starts:
        copy.start()
    stokes_all[gp] = profile_ref[...]
    return waits


def middle_kernel(n, g, width, flow_ref, profile_ref, edge_ref, flow_out, drift_out, halo_out,
                  west_flow, east_flow, stokes_all, halo, sems, psend, precv, halo_sems):
    me, gp = lax.axis_index("comp"), lax.axis_index("grp")
    levels = flow_ref.shape[0] // 2
    lanes = profile_ref.shape[1]
    height = lanes // width
    greet(n, g, me, gp, False)
    right, left = lax.rem(me + 1, n), lax.rem(me + n - 1, n)
    up, down = lax.rem(gp + 1, g), lax.rem(gp + g - 1, g)
    a, b, c, d = height, 2 * height, 2 * height + width, 2 * height + 2 * width
    waits = ocean_copies(n, g, me, gp, flow_ref, profile_ref, west_flow, east_flow, stokes_all, sems, psend, precv)
    moves = [
        remote(edge_ref.at[a:b], halo.at[0:a], halo_sems.at[0], halo_sems.at[1], (right, gp)),
        remote(edge_ref.at[0:a], halo.at[a:b], halo_sems.at[2], halo_sems.at[3], (left, gp)),
        remote(edge_ref.at[c:d], halo.at[b:c], halo_sems.at[4], halo_sems.at[5], (me, up)),
        remote(edge_ref.at[b:c], halo.at[c:d], halo_sems.at[6], halo_sems.at[7], (me, down)),
    ]
    for copy in moves:
        copy.start()
    for copy in waits:
        copy.wait()
    stokes = jnp.concatenate([stokes_all[i] for i in range(g)], axis=1)
    new_x, new_y = ocean_step(width, flow_ref[...], west_flow[...], east_flow[...], stokes, me == 0, me == n - 1)
    flow_out[:levels, :] = new_x
    flow_out[levels:, :] = new_y
    here = pl.ds(pl.multiple_of(gp * lanes, lanes), lanes)
    drift_out[0:1, :] = CURRENT_GAIN * jnp.tanh(flow_out[0:1, here])
    drift_out[1:2, :] = CURRENT_GAIN * jnp.tanh(flow_out[levels:levels + 1, here])
    for copy in moves:
        copy.wait()
    halo_out[0:a, :] = jnp.where(me == 0, 0.0, halo[0:a, :])
    halo_out[a:b, :] = jnp.where(me == n - 1, 0.0, halo[a:b, :])
    halo_out[b:c, :] = jnp.where(gp == 0, 0.0, halo[b:c, :])
    halo_out[c:d, :] = jnp.where(gp == g - 1, 0.0, halo[c:d, :])


def exit_kernel(n, g, width, points_ref, flow_ref, profile_ref, out_ref, flow_out,
                west_flow, east_flow, stokes_all, blocks, sems, psend, precv, sends, recvs):
    me, gp = lax.axis_index("comp"), lax.axis_index("grp")
    levels = flow_ref.shape[0] // 2
    kept, rows, cols = out_ref.shape
    lanes = blocks.shape[2]
    greet(n, g, me, gp, True)
    waits = ocean_copies(n, g, me, gp, flow_ref, profile_ref, west_flow, east_flow, stokes_all, sems, psend, precv)
    for i in range(1, n):
        peer = lax.rem(me + i, n)
        remote(points_ref.at[peer], blocks.at[me], sends.at[peer], recvs.at[me], (peer, gp)).start()
    blocks[me] = points_ref[me]
    for copy in waits:
        copy.wait()
    stokes = jnp.concatenate([stokes_all[i] for i in range(g)], axis=1)
    new_x, new_y = ocean_step(width, flow_ref[...], west_flow[...], east_flow[...], stokes, me == 0, me == n - 1)
    flow_out[:levels, :] = new_x
    flow_out[levels:, :] = new_y
    for i in range(1, n):
        peer = lax.rem(me + i, n)
        remote(points_ref.at[peer], blocks.at[peer], sends.at[peer], recvs.at[peer], (peer, gp)).wait()
    for h in range(cols // lanes):
        turned = jnp.swapaxes(blocks[h * rows:(h + 1) * rows], 0, 1)
        out_ref[:, :, h * lanes:(h + 1) * lanes] = swap_blocks(turned)


VMEM = pltpu.VMEM
DMA = pltpu.SemaphoreType.DMA


def call(kernel, operands, outs, scratch, collective=None):
    whole = pl.BlockSpec(memory_space=pltpu.VMEM)
    extra = {} if collective is None else {"collective_id": collective, "has_side_effects": True}
    return pl.pallas_call(
        kernel,
        out_shape=tuple(jax.ShapeDtypeStruct(shape, jnp.float32) for shape in outs),
        in_specs=[whole] * len(operands),
        out_specs=(whole,) * len(outs),
        scratch_shapes=scratch,
        compiler_params=pltpu.CompilerParams(vmem_limit_bytes=(24 if collective is None else 16) * 1024 * 1024, **extra),
    )(*operands)


def local(spectrum, group_speed, sea_mask, quad_index, coupling, stokes_kernel, ocean_flow):
    f32 = jnp.float32
    n, g = lax.axis_size("comp"), lax.axis_size("grp")
    kept, rows, cols = spectrum.shape
    width = ocean_flow.shape[3]
    lanes = rows * width
    channels, quads = coupling.shape
    place = lax.axis_index("comp")
    flow = ocean_flow.reshape(2 * L, -1)
    deep, size = flow.shape
    own = lax.dynamic_slice_in_dim(group_speed, place * kept, kept, 1)
    own = jnp.broadcast_to(own[:, :, None, None], (2, kept, rows, lanes))
    wet_flat = (lax.dynamic_slice_in_dim(sea_mask, place * width, width, 1) == 1).astype(f32).reshape(1, lanes)
    edges = 2 * rows + 2 * width
    chunk = 128 if quads % 128 == 0 else quads
    work = [
        VMEM((quads // chunk, 4 * chunk, channels), jnp.bfloat16),
        VMEM((channels, 2 * lanes), jnp.bfloat16),
        VMEM((quads, lanes), jnp.bfloat16),
    ]
    sea = [VMEM((deep, size), f32), VMEM((deep, size), f32), VMEM((g, deep, lanes), f32)]

    (points,) = call(
        functools.partial(enter_kernel, n, g), (spectrum, flow, own, sea_mask), ((n, kept, lanes),),
        [VMEM((kept, rows, cols), f32), VMEM((kept, rows, cols), f32), VMEM((2, lanes), f32),
         VMEM((n, 2, lanes), f32), VMEM((n, kept, lanes), f32), DMA((2, n)), DMA((2, n)), DMA((4,))], 0,
    )
    fixed = (quad_index, coupling, stokes_kernel, wet_flat)
    points, profile, edge = call(
        functools.partial(source_kernel, False, rows), (points.reshape(channels, lanes), *fixed),
        ((channels, lanes), (deep, lanes), (edges, channels)), work,
    )
    flow, drift, halo = call(
        functools.partial(middle_kernel, n, g, width), (flow, profile, edge),
        ((deep, size), (2, lanes), (edges, channels)),
        sea + [VMEM((edges, channels), f32), DMA((4,)), DMA((g,)), DMA((g,)), DMA((8,))], 1,
    )
    points, profile = call(
        functools.partial(source_kernel, True, rows), (points, *fixed, halo, group_speed.T, drift),
        ((channels, lanes), (deep, lanes)), work,
    )
    energy, flow = call(
        functools.partial(exit_kernel, n, g, width), (points.reshape(n, kept, lanes), flow, profile),
        ((kept, rows, cols), (deep, size)),
        sea + [VMEM((n, kept, lanes), f32), DMA((4,)), DMA((g,)), DMA((g,)), DMA((n,)), DMA((n,))], 2,
    )
    return (energy, flow.reshape(ocean_flow.shape))


def solution(mesh):
    in_specs = (
        P("comp", "grp", None),
        P(),
        P("grp", None),
        P(),
        P(),
        P(),
        P(None, None, None, "comp"),
    )
    out_specs = (P("comp", "grp", None), P(None, None, None, "comp"))
    return jax.shard_map(local, mesh=mesh, in_specs=in_specs, out_specs=out_specs, check_vma=False)
```
